32 devices in a mesh: owner: 8 (over z, y), blk: 4 (over x, core).
Axes of the slice: x: 2, y: 2, z: 4, core: 2. Of those that a mesh axis runs over, the one named last changes fastest.
Arguments:
- entity_table: bfloat16 [32768, 256], P('owner'), may hold values from -1.5 to 1.5
- relations: bfloat16 [8, 256, 256], replicated, may hold values from -0.375 to 0.375
- head_ids: int32 [32768], P(('owner', 'blk')), may hold values from 0 to 32767, as said below
- rel_ids: int32 [32768], P(('owner', 'blk')), may hold values from 0 to 7
- tail_ids: int32 [32768], P(('owner', 'blk')), may hold values from 0 to 32767, as said below
- neg_ids: int32 [16384], P(('owner', 'blk')), may hold values from 0 to 32767, as said below
Outputs:
- entity_grad: float32 [32768, 256], P(('owner', 'blk'))
- relation_grad: float32 [8, 256, 256], P('blk')
The draws below stay inside these ranges and needn't reach their ends.
Inputs may be any that keep to these rules, and one draw needn't show every extreme that they name: An entity is held by the owner index whose shard of entity_table contains its row. A device's ids are its own shards of head_ids, tail_ids and neg_ids together. Of these ids every owner holds at most 800 (800), and some owner holds exactly 800; that owner is the same for all devices of one blk index. `tail_ids`: as for head_ids: the same bound of 800 ids of one device for one owner, over the device's heads, tails and negatives together. `neg_ids`: as for head_ids: the same bound of 800 ids of one device for one owner, over the device's heads, tails and negatives together.
All inputs are finite; a program needn't handle non-finite values.
Results may differ from the reference program's by a relative error of at most 0.0027.
Values may be sent and summed in bfloat16 or wider, within the bound.
A program may use at most 64 MiB of HBM per device.

```python
import jax
import jax.numpy as jnp
from jax import lax

D = 256
REL = 8
ENT_DEV = 4096
TRI = 1024
NEG = 512
CAP = 800
ENTITIES = 32768
TRIPLES = 32768
N_OWNER = 8
N_BLK = 4


def entity_draw(key):
    subkeys = jax.random.split(jax.random.fold_in(key, 7321), 4)
    devices_all = N_OWNER * N_BLK
    wanted_count = 2 * TRI + NEG
    rest_count = wanted_count - CAP
    hot_owner = jax.random.randint(subkeys[0], (N_BLK,), 0, N_OWNER)
    device_hot = jnp.tile(hot_owner, N_OWNER)
    position = jnp.arange(rest_count, dtype=jnp.int32)
    nudges = jax.random.randint(subkeys[1], (devices_all, rest_count), 0, 2)
    others = (position[None, :] % (N_OWNER - 1) + nudges) % (N_OWNER - 1)
    others = others + (others >= device_hot[:, None]).astype(jnp.int32)
    hot_part = jnp.broadcast_to(device_hot[:, None], (devices_all, CAP)).astype(jnp.int32)
    owner_labels = jnp.concatenate([hot_part, others.astype(jnp.int32)], axis=1)
    order_keys = jax.random.randint(subkeys[2], (devices_all, wanted_count), 0, wanted_count) * wanted_count
    order_keys = order_keys + jnp.arange(wanted_count, dtype=jnp.int32)[None, :]
    order = jnp.argsort(order_keys, axis=1, stable=True)
    owner_labels = jnp.take_along_axis(owner_labels, order, axis=1)
    local_rows = jax.random.randint(subkeys[3], (devices_all, wanted_count), 0, ENT_DEV)
    return (owner_labels * ENT_DEV + local_rows).astype(jnp.int32)


def draw_head_ids(key, part):
    return entity_draw(key)[:, :TRI].reshape(-1)


def draw_tail_ids(key, part):
    return entity_draw(key)[:, TRI:2 * TRI].reshape(-1)


def draw_neg_ids(key, part):
    return entity_draw(key)[:, 2 * TRI:].reshape(-1)


def plant(entries, own_key, least, high):
    place = [jax.random.randint(jax.random.fold_in(own_key, axis), (), 0, length) for axis, length in enumerate(entries.shape)]
    main_axis = entries.shape.index(max(entries.shape))
    next_to = place[:main_axis] + [(place[main_axis] + 1) % entries.shape[main_axis]] + place[main_axis + 1:]
    return entries.at[tuple(place)].set(least).at[tuple(next_to)].set(high)


def shard_levels(rng, extent, pieces, smallest, largest):
    gain, own = 1.0, jax.random.fold_in(rng, 6)
    for dim, parts in pieces:
        draws = jnp.exp(jax.random.uniform(jax.random.fold_in(own, dim), (parts,), jnp.float32, smallest / len(pieces), largest / len(pieces)))
        gain = gain * jnp.repeat(draws, extent[dim] // parts).reshape([-1 if axis == dim else 1 for axis in range(len(extent))])
    return gain


def noise(rng, shape, width, limit, shards=(), kind=jnp.bfloat16):
    array = jax.random.normal(rng, shape, jnp.float32) * width
    if len(shards) > 0:
        array = shard_levels(rng, shape, shards, -0.22, 0.18) * array
    return jnp.clip(array, min=-limit, max=limit).astype(kind)


def setup_inputs(seed: int = 0) -> dict:
    splits = jax.random.split(jax.random.key(seed), 7)
    return {
        "entity_table": noise(splits[0], (ENTITIES, D), 0.25, 1.5, ((0, 8),)),
        "relations": noise(splits[1], (REL, D, D), D ** -0.5, 0.375),
        "head_ids": draw_head_ids(jax.random.fold_in(splits[6], 71), 0),
        "rel_ids": plant(jax.random.randint(splits[3], (TRIPLES,), 0, REL), jax.random.fold_in(splits[3], 1), 0, REL - 1).astype(jnp.int32),
        "tail_ids": draw_tail_ids(jax.random.fold_in(splits[6], 71), 0),
        "neg_ids": draw_neg_ids(jax.random.fold_in(splits[6], 71), 0),
    }


def reference(entity_table, relations, head_ids, rel_ids, tail_ids, neg_ids):
    neg_scale = (N_BLK * NEG) ** -0.5
    group_inputs = (head_ids.reshape(N_OWNER, N_BLK * TRI), rel_ids.reshape(N_OWNER, N_BLK * TRI),
                    tail_ids.reshape(N_OWNER, N_BLK * TRI), neg_ids.reshape(N_OWNER, N_BLK * NEG))

    def group_step(totals, inputs):
        entity_grad, relation_grad = totals
        head_index, relation_index, tail_index, negative_index = inputs
        head_rows = entity_table[head_index]
        tail_rows = entity_table[tail_index]
        negative_rows = entity_table[negative_index]
        queries = jnp.zeros((N_BLK * TRI, D), jnp.float32)
        for relation in range(REL):
            chosen = (relation_index == relation)[:, None]
            queries = queries + jnp.where(chosen, jnp.dot(head_rows, relations[relation], preferred_element_type=jnp.float32), 0.0)
        queries = queries.astype(jnp.bfloat16)
        positive = jnp.sum(queries.astype(jnp.float32) * tail_rows.astype(jnp.float32), axis=1)
        slopes = -jax.nn.sigmoid(-positive)
        scores = jnp.dot(queries, negative_rows.T, preferred_element_type=jnp.float32)
        weights = (neg_scale * jax.nn.sigmoid(scores)).astype(jnp.bfloat16)
        partners = (slopes[:, None] * tail_rows.astype(jnp.float32)
                    + jnp.dot(weights, negative_rows, preferred_element_type=jnp.float32)).astype(jnp.bfloat16)
        neg_grads = jnp.dot(weights.T, queries, preferred_element_type=jnp.float32)
        tail_grads = slopes[:, None] * queries.astype(jnp.float32)
        head_grads = jnp.zeros((N_BLK * TRI, D), jnp.float32)
        stacked = []
        for relation in range(REL):
            chosen = (relation_index == relation)[:, None]
            head_grads = head_grads + jnp.where(chosen, jnp.dot(partners, relations[relation].T, preferred_element_type=jnp.float32), 0.0)
            masked_heads = head_rows * chosen.astype(jnp.bfloat16)
            stacked.append(jnp.dot(masked_heads.T, partners, preferred_element_type=jnp.float32))
        entity_grad = entity_grad.at[head_index].add(head_grads)
        entity_grad = entity_grad.at[tail_index].add(tail_grads)
        entity_grad = entity_grad.at[negative_index].add(neg_grads)
        return (entity_grad, relation_grad + jnp.stack(stacked)), None

    start_totals = (jnp.zeros((ENTITIES, D), jnp.float32), jnp.zeros((REL, D, D), jnp.float32))
    (entity_grad, relation_grad), unused = lax.scan(group_step, start_totals, group_inputs)
    return (entity_grad, relation_grad)
```

```python
import jax
import jax.numpy as jnp
from jax import lax
from jax.sharding import PartitionSpec as P


def passed_along(block, axis, distance):
    devices = range(lax.axis_size(axis))
    route = [((i - distance) % len(devices), i) for i in devices]
    return lax.ppermute(block, axis, route)


def earlier(count):
    place = jnp.arange(count, dtype=jnp.int32)
    return (place[:, None] > place[None, :]).astype(jnp.bfloat16)


def ranks(onehot):
    ids, owner_count = onehot.shape
    run = 128
    runs = onehot.reshape(ids // run, run, owner_count)
    within = jnp.einsum("ij,bjo->bio", earlier(run), runs, preferred_element_type=jnp.float32)
    totals = jnp.sum(runs.astype(jnp.float32), axis=1).astype(jnp.bfloat16)
    carried = jnp.dot(earlier(ids // run), totals, preferred_element_type=jnp.float32)
    before = within + carried[:, None, :]
    return jnp.sum(before * runs.astype(jnp.float32), axis=2).reshape(ids).astype(jnp.int32)


def shards(entity_table, relations, head_ids, rel_ids, tail_ids, neg_ids):
    owner_count = lax.axis_size("owner")
    cycle_count = lax.axis_size("blk")
    entity_rows, feature_count = entity_table.shape
    triple_count = head_ids.shape[0]
    negative_count = neg_ids.shape[0]
    relation_count = relations.shape[0]
    wanted = jnp.concatenate([head_ids, tail_ids, neg_ids])
    wanted_count = wanted.shape[0]
    capacity = 5 * wanted_count // (2 * owner_count)
    owners = wanted // entity_rows
    local_rows = wanted % entity_rows
    onehot = (owners[:, None] == jnp.arange(owner_count, dtype=jnp.int32)[None, :]).astype(
        jnp.bfloat16
    )
    slot_index = ranks(onehot)
    target = owners * capacity + slot_index
    slots = jnp.arange(owner_count * capacity, dtype=jnp.int32)
    packing = (slots[:, None] == target[None, :]).astype(jnp.bfloat16)
    digits = jnp.stack([local_rows // 64, local_rows % 64], axis=1).astype(jnp.bfloat16)
    packed = jnp.dot(packing, digits, preferred_element_type=jnp.float32).astype(jnp.int32)
    requests = (packed[:, 0] * 64 + packed[:, 1]).reshape(owner_count, capacity)
    asked_rows = lax.all_to_all(requests, "owner", split_axis=0, concat_axis=0, tiled=True)
    found_rows = jnp.take(entity_table, asked_rows, axis=0)
    fetched, asked_rows = (
        lax.all_to_all(found_rows, "owner", split_axis=0, concat_axis=0, tiled=True),
        asked_rows,
    )
    fetched_rows = fetched.reshape(owner_count * capacity, feature_count)[target]
    head_rows = fetched_rows[:triple_count]
    tail_rows = fetched_rows[triple_count : 2 * triple_count]
    negative_rows = fetched_rows[2 * triple_count :]
    relation_hot = (
        rel_ids[:, None] == jnp.arange(relation_count, dtype=jnp.int32)[None, :]
    ).astype(jnp.bfloat16)
    spread_heads = (head_rows[:, None, :] * relation_hot[:, :, None]).reshape(
        triple_count, relation_count * feature_count
    )
    flat_relations = relations.reshape(relation_count * feature_count, feature_count)
    queries = jnp.dot(spread_heads, flat_relations, preferred_element_type=jnp.float32).astype(
        jnp.bfloat16
    )
    positive = jnp.einsum("id,id->i", queries, tail_rows, preferred_element_type=jnp.float32)
    slopes = -jax.nn.sigmoid(-positive)
    scale_neg = (cycle_count * negative_count) ** (-0.5)
    partner = slopes[:, None] * tail_rows.astype(jnp.float32)
    contract_rows = (((0,), (0,)), ((), ()))
    contract_cols = (((1,), (1,)), ((), ()))
    travelling = negative_rows
    collected = jnp.zeros((negative_count, feature_count), jnp.float32)
    for turn_index in range(cycle_count):
        scores = lax.dot_general(
            queries, travelling, contract_cols, preferred_element_type=jnp.float32
        )
        weights = (scale_neg * jax.nn.sigmoid(scores)).astype(jnp.bfloat16)
        partner = partner + jnp.dot(weights, travelling, preferred_element_type=jnp.float32)
        collected = collected + lax.dot_general(
            weights, queries, contract_rows, preferred_element_type=jnp.float32
        )
        if turn_index + 1 < cycle_count:
            travelling = passed_along(travelling, "blk", 1)
        collected = passed_along(collected, "blk", 1)
    partner_low = partner.astype(jnp.bfloat16)
    spread_partner = partner_low[:, None, :] * relation_hot[:, :, None]
    head_grad = jnp.einsum(
        "ire,rde->id", spread_partner, relations, preferred_element_type=jnp.float32
    )
    tail_grad = slopes[:, None] * queries.astype(jnp.float32)
    rel_term = lax.dot_general(
        spread_heads, partner_low, contract_rows, preferred_element_type=jnp.float32
    )
    rel_term = rel_term.reshape(relation_count, feature_count, feature_count)
    row_grads = jnp.concatenate([head_grad, tail_grad, collected], axis=0)
    outgoing = jnp.dot(
        packing, row_grads.astype(jnp.bfloat16), preferred_element_type=jnp.float32
    ).astype(jnp.bfloat16)
    outgoing = outgoing.reshape(owner_count, capacity, feature_count)
    returned = lax.all_to_all(outgoing, "owner", split_axis=0, concat_axis=0, tiled=True)
    landing = (
        jnp.arange(entity_rows, dtype=jnp.int32)[:, None] == asked_rows.reshape(-1)[None, :]
    ).astype(jnp.bfloat16)
    shard_grad = jnp.dot(
        landing, returned.reshape(-1, feature_count), preferred_element_type=jnp.float32
    )
    ent_grad = lax.psum_scatter(shard_grad, "blk", scatter_dimension=0, tiled=True)
    summed_group = lax.psum_scatter(rel_term, "blk", scatter_dimension=0, tiled=True)
    rel_grad = lax.psum(summed_group, "owner")
    return (ent_grad, rel_grad)


def solution(mesh):
    placed = (
        P("owner", None),
        P(),
        P(("owner", "blk")),
        P(("owner", "blk")),
        P(("owner", "blk")),
        P(("owner", "blk")),
    )
    return jax.shard_map(
        shards,
        mesh=mesh,
        in_specs=placed,
        out_specs=(P(("owner", "blk"), None), P("blk", None, None)),
        check_vma=False,
    )
```

```python
import jax
import jax.numpy as jnp
from jax import lax
from jax.sharding import PartitionSpec as P


def passed_along(block, axis, distance):
    devices = range(lax.axis_size(axis))
    route = [((i - distance) % len(devices), i) for i in devices]
    return lax.ppermute(block, axis, route)


def earlier(count):
    place = jnp.arange(count, dtype=jnp.int32)
    return (place[:, None] > place[None, :]).astype(jnp.bfloat16)


def ranks(onehot):
    ids, owner_count = onehot.shape
    run = 128
    runs = onehot.reshape(ids // run, run, owner_count)
    within = jnp.einsum("ij,bjo->bio", earlier(run), runs, preferred_element_type=jnp.float32)
    totals = jnp.sum(runs.astype(jnp.float32), axis=1).astype(jnp.bfloat16)
    carried = jnp.dot(earlier(ids // run), totals, preferred_element_type=jnp.float32)
    before = within + carried[:, None, :]
    return jnp.sum(before * runs.astype(jnp.float32), axis=2).reshape(ids).astype(jnp.int32)


def group_sums(rows, grads, entity_rows):
    members = lax.axis_size("blk")
    pairs = members // 2
    size = entity_rows // members
    me = lax.axis_index("blk")
    pair, core = me // 2, me % 2
    swap = [(i, i ^ 1) for i in range(members)]

    def block(index):
        wanted = index * size + jnp.arange(size, dtype=jnp.int32)
        landing = (wanted[:, None] == rows[None, :]).astype(jnp.bfloat16)
        return jnp.dot(landing, grads, preferred_element_type=jnp.float32)

    arrived = []
    for step in range(1, pairs + 1):
        target = (pair + step) % pairs
        other = lax.ppermute(block(2 * target + 1 - core), "blk", swap)
        total = block(2 * target + core) + other
        if step < pairs:
            route = [(i, (i + 2 * step) % members) for i in range(members)]
            arrived.append(lax.ppermute(total.astype(jnp.bfloat16), "blk", route))
    for part in arrived:
        total = total + part.astype(jnp.float32)
    return total


def shards(entity_table, relations, head_ids, rel_ids, tail_ids, neg_ids):
    owner_count = lax.axis_size("owner")
    cycle_count = lax.axis_size("blk")
    entity_rows, feature_count = entity_table.shape
    triple_count = head_ids.shape[0]
    negative_count = neg_ids.shape[0]
    relation_count = relations.shape[0]
    wanted = jnp.concatenate([head_ids, tail_ids, neg_ids])
    wanted_count = wanted.shape[0]
    capacity = 5 * wanted_count // (2 * owner_count)
    owners = wanted // entity_rows
    local_rows = wanted % entity_rows
    onehot = (owners[:, None] == jnp.arange(owner_count, dtype=jnp.int32)[None, :]).astype(
        jnp.bfloat16
    )
    slot_index = ranks(onehot)
    target = owners * capacity + slot_index
    slots = jnp.arange(owner_count * capacity, dtype=jnp.int32)
    packing = (slots[:, None] == target[None, :]).astype(jnp.bfloat16)
    digits = jnp.stack([local_rows // 64, local_rows % 64], axis=1).astype(jnp.bfloat16)
    packed = jnp.dot(packing, digits, preferred_element_type=jnp.float32).astype(jnp.int32)
    requests = (packed[:, 0] * 64 + packed[:, 1]).reshape(owner_count, capacity)
    asked_rows = lax.all_to_all(requests, "owner", split_axis=0, concat_axis=0, tiled=True)
    found_rows = jnp.take(entity_table, asked_rows, axis=0)
    fetched, asked_rows = (
        lax.all_to_all(found_rows, "owner", split_axis=0, concat_axis=0, tiled=True),
        asked_rows,
    )
    fetched_rows = fetched.reshape(owner_count * capacity, feature_count)[target]
    head_rows = fetched_rows[:triple_count]
    tail_rows = fetched_rows[triple_count : 2 * triple_count]
    negative_rows = fetched_rows[2 * triple_count :]
    relation_hot = (
        rel_ids[:, None] == jnp.arange(relation_count, dtype=jnp.int32)[None, :]
    ).astype(jnp.bfloat16)
    spread_heads = (head_rows[:, None, :] * relation_hot[:, :, None]).reshape(
        triple_count, relation_count * feature_count
    )
    flat_relations = relations.reshape(relation_count * feature_count, feature_count)
    queries = jnp.dot(spread_heads, flat_relations, preferred_element_type=jnp.float32).astype(
        jnp.bfloat16
    )
    positive = jnp.einsum("id,id->i", queries, tail_rows, preferred_element_type=jnp.float32)
    slopes = -jax.nn.sigmoid(-positive)
    scale_neg = (cycle_count * negative_count) ** (-0.5)
    partner = slopes[:, None] * tail_rows.astype(jnp.float32)
    contract_rows = (((0,), (0,)), ((), ()))
    contract_cols = (((1,), (1,)), ((), ()))
    travelling = negative_rows
    collected = jnp.zeros((negative_count, feature_count), jnp.float32)
    for turn_index in range(cycle_count):
        scores = lax.dot_general(
            queries, travelling, contract_cols, preferred_element_type=jnp.float32
        )
        weights = (scale_neg * jax.nn.sigmoid(scores)).astype(jnp.bfloat16)
        partner = partner + jnp.dot(weights, travelling, preferred_element_type=jnp.float32)
        collected = collected + lax.dot_general(
            weights, queries, contract_rows, preferred_element_type=jnp.float32
        )
        if turn_index + 1 < cycle_count:
            travelling = passed_along(travelling, "blk", 1)
        collected = passed_along(collected, "blk", 1)
    partner_low = partner.astype(jnp.bfloat16)
    spread_partner = partner_low[:, None, :] * relation_hot[:, :, None]
    head_grad = jnp.einsum(
        "ire,rde->id", spread_partner, relations, preferred_element_type=jnp.float32
    )
    tail_grad = slopes[:, None] * queries.astype(jnp.float32)
    rel_term = lax.dot_general(
        spread_heads, partner_low, contract_rows, preferred_element_type=jnp.float32
    )
    rel_term = rel_term.reshape(relation_count, feature_count, feature_count)
    row_grads = jnp.concatenate([head_grad, tail_grad, collected], axis=0)
    outgoing = jnp.dot(
        packing, row_grads.astype(jnp.bfloat16), preferred_element_type=jnp.float32
    ).astype(jnp.bfloat16)
    outgoing = outgoing.reshape(owner_count, capacity, feature_count)
    returned = lax.all_to_all(outgoing, "owner", split_axis=0, concat_axis=0, tiled=True)
    ent_grad = group_sums(asked_rows.reshape(-1), returned.reshape(-1, feature_count), entity_rows)
    summed_group = lax.psum_scatter(rel_term, "blk", scatter_dimension=0, tiled=True)
    gathered = lax.all_gather(summed_group.astype(jnp.bfloat16), "owner")
    rel_grad = jnp.sum(gathered.astype(jnp.float32), axis=0)
    return (ent_grad, rel_grad)


def solution(mesh):
    placed = (
        P("owner", None),
        P(),
        P(("owner", "blk")),
        P(("owner", "blk")),
        P(("owner", "blk")),
        P(("owner", "blk")),
    )
    return jax.shard_map(
        shards,
        mesh=mesh,
        in_specs=placed,
        out_specs=(P(("owner", "blk"), None), P("blk", None, None)),
        check_vma=False,
    )
```

```python
import jax
import jax.numpy as jnp
from jax import lax
from jax.sharding import PartitionSpec as P


def earlier(count):
    place = jnp.arange(count, dtype=jnp.int32)
    return (place[:, None] > place[None, :]).astype(jnp.bfloat16)


def ranks(onehot):
    ids, owner_count = onehot.shape
    run = 128
    runs = onehot.reshape(ids // run, run, owner_count)
    within = jnp.einsum("ij,bjo->bio", earlier(run), runs, preferred_element_type=jnp.float32)
    totals = jnp.sum(runs.astype(jnp.float32), axis=1).astype(jnp.bfloat16)
    carried = jnp.dot(earlier(ids // run), totals, preferred_element_type=jnp.float32)
    before = within + carried[:, None, :]
    return jnp.sum(before * runs.astype(jnp.float32), axis=2).reshape(ids).astype(jnp.int32)


def group_sums(rows, grads, entity_rows):
    members = lax.axis_size("blk")
    pairs = members // 2
    size = entity_rows // members
    me = lax.axis_index("blk")
    pair, core = me // 2, me % 2
    swap = [(i, i ^ 1) for i in range(members)]

    def block(index):
        wanted = index * size + jnp.arange(size, dtype=jnp.int32)
        landing = (wanted[:, None] == rows[None, :]).astype(jnp.bfloat16)
        return jnp.dot(landing, grads, preferred_element_type=jnp.float32)

    arrived = []
    for step in range(1, pairs + 1):
        target = (pair + step) % pairs
        other = lax.ppermute(block(2 * target + 1 - core), "blk", swap)
        total = block(2 * target + core) + other
        if step < pairs:
            route = [(i, (i + 2 * step) % members) for i in range(members)]
            arrived.append(lax.ppermute(total.astype(jnp.bfloat16), "blk", route))
    for part in arrived:
        total = total + part.astype(jnp.float32)
    return total


def shards(entity_table, relations, head_ids, rel_ids, tail_ids, neg_ids):
    owner_count = lax.axis_size("owner")
    cycle_count = lax.axis_size("blk")
    entity_rows, feature_count = entity_table.shape
    triple_count = head_ids.shape[0]
    negative_count = neg_ids.shape[0]
    relation_count = relations.shape[0]
    wanted = jnp.concatenate([head_ids, tail_ids, neg_ids])
    wanted_count = wanted.shape[0]
    capacity = 5 * wanted_count // (2 * owner_count)
    owners = wanted // entity_rows
    local_rows = wanted % entity_rows
    onehot = (owners[:, None] == jnp.arange(owner_count, dtype=jnp.int32)[None, :]).astype(
        jnp.bfloat16
    )
    slot_index = ranks(onehot)
    target = owners * capacity + slot_index
    slots = jnp.arange(owner_count * capacity, dtype=jnp.int32)
    packing = (slots[:, None] == target[None, :]).astype(jnp.bfloat16)
    digits = jnp.stack([local_rows // 64, local_rows % 64], axis=1).astype(jnp.bfloat16)
    packed = jnp.dot(packing, digits, preferred_element_type=jnp.float32).astype(jnp.int32)
    requests = (packed[:, 0] * 64 + packed[:, 1]).reshape(owner_count, capacity)
    asked_rows = lax.all_to_all(requests, "owner", split_axis=0, concat_axis=0, tiled=True)
    found_rows = entity_table.at[asked_rows].get(mode="promise_in_bounds")
    fetched, asked_rows = (
        lax.all_to_all(found_rows, "owner", split_axis=0, concat_axis=0, tiled=True),
        asked_rows,
    )
    fetched_rows = fetched.reshape(owner_count * capacity, feature_count)
    fetched_rows = fetched_rows.at[target].get(mode="promise_in_bounds")
    head_rows = fetched_rows[:triple_count]
    tail_rows = fetched_rows[triple_count : 2 * triple_count]
    negative_rows = fetched_rows[2 * triple_count :]
    routes = [[(i, i ^ step) for i in range(cycle_count)] for step in range(cycle_count)]
    visitors = [negative_rows]
    for step in range(1, cycle_count):
        visitors.append(lax.ppermute(negative_rows, "blk", routes[step]))
    relation_hot = (
        rel_ids[:, None] == jnp.arange(relation_count, dtype=jnp.int32)[None, :]
    ).astype(jnp.bfloat16)
    spread_heads = (head_rows[:, None, :] * relation_hot[:, :, None]).reshape(
        triple_count, relation_count * feature_count
    )
    flat_relations = relations.reshape(relation_count * feature_count, feature_count)
    queries = jnp.dot(spread_heads, flat_relations, preferred_element_type=jnp.float32).astype(
        jnp.bfloat16
    )
    positive = jnp.einsum("id,id->i", queries, tail_rows, preferred_element_type=jnp.float32)
    slopes = -jax.nn.sigmoid(-positive)
    scale_neg = (cycle_count * negative_count) ** (-0.5)
    partner = slopes[:, None] * tail_rows.astype(jnp.float32)
    contract_rows = (((0,), (0,)), ((), ()))
    contract_cols = (((1,), (1,)), ((), ()))
    returning = []
    for step, visitor in enumerate(visitors):
        scores = lax.dot_general(
            queries, visitor, contract_cols, preferred_element_type=jnp.float32
        )
        weights = (scale_neg * jax.nn.sigmoid(scores)).astype(jnp.bfloat16)
        partner = partner + jnp.dot(weights, visitor, preferred_element_type=jnp.float32)
        sums = lax.dot_general(weights, queries, contract_rows, preferred_element_type=jnp.float32)
        if step == 0:
            collected = sums
        else:
            returning.append(lax.ppermute(sums.astype(jnp.bfloat16), "blk", routes[step]))
    partner_low = partner.astype(jnp.bfloat16)
    spread_partner = partner_low[:, None, :] * relation_hot[:, :, None]
    head_grad = jnp.einsum(
        "ire,rde->id", spread_partner, relations, preferred_element_type=jnp.float32
    )
    tail_grad = slopes[:, None] * queries.astype(jnp.float32)
    rel_term = lax.dot_general(
        spread_heads, partner_low, contract_rows, preferred_element_type=jnp.float32
    )
    rel_term = rel_term.reshape(relation_count, feature_count, feature_count)
    triple_grads = jnp.concatenate([head_grad, tail_grad], axis=0).astype(jnp.bfloat16)
    outgoing = jnp.dot(
        packing[:, : 2 * triple_count], triple_grads, preferred_element_type=jnp.float32
    ).astype(jnp.bfloat16)
    for part in returning:
        collected = collected + part.astype(jnp.float32)
    outgoing = outgoing + jnp.dot(
        packing[:, 2 * triple_count :],
        collected.astype(jnp.bfloat16),
        preferred_element_type=jnp.float32,
    ).astype(jnp.bfloat16)
    outgoing = outgoing.reshape(owner_count, capacity, feature_count)
    returned = lax.all_to_all(outgoing, "owner", split_axis=0, concat_axis=0, tiled=True)
    ent_grad = group_sums(asked_rows.reshape(-1), returned.reshape(-1, feature_count), entity_rows)
    summed_group = lax.psum_scatter(rel_term, "blk", scatter_dimension=0, tiled=True)
    gathered = lax.all_gather(summed_group.astype(jnp.bfloat16), "owner")
    rel_grad = jnp.sum(gathered.astype(jnp.float32), axis=0)
    return (ent_grad, rel_grad)


def solution(mesh):
    placed = (
        P("owner", None),
        P(),
        P(("owner", "blk")),
        P(("owner", "blk")),
        P(("owner", "blk")),
        P(("owner", "blk")),
    )
    return jax.shard_map(
        shards,
        mesh=mesh,
        in_specs=placed,
        out_specs=(P(("owner", "blk"), None), P("blk", None, None)),
        check_vma=False,
    )
```

```python
import jax
import jax.numpy as jnp
from jax import lax
from jax.sharding import PartitionSpec as P


def earlier(count):
    place = jnp.arange(count, dtype=jnp.int32)
    return (place[:, None] > place[None, :]).astype(jnp.bfloat16)


def ranks(onehot):
    ids, owner_count = onehot.shape
    run = 128
    runs = onehot.reshape(ids // run, run, owner_count)
    within = jnp.einsum("ij,bjo->bio", earlier(run), runs, preferred_element_type=jnp.float32)
    totals = jnp.sum(runs.astype(jnp.float32), axis=1).astype(jnp.bfloat16)
    carried = jnp.dot(earlier(ids // run), totals, preferred_element_type=jnp.float32)
    before = within + carried[:, None, :]
    return jnp.sum(before * runs.astype(jnp.float32), axis=2).reshape(ids).astype(jnp.int32)


def group_sums(rows, grads, entity_rows):
    members = lax.axis_size("blk")
    pairs = members // 2
    size = entity_rows // members
    me = lax.axis_index("blk")
    pair, core = me // 2, me % 2
    swap = [(i, i ^ 1) for i in range(members)]

    def block(index):
        wanted = index * size + jnp.arange(size, dtype=jnp.int32)
        landing = (wanted[:, None] == rows[None, :]).astype(jnp.bfloat16)
        return jnp.dot(landing, grads, preferred_element_type=jnp.float32)

    arrived = []
    for step in range(1, pairs + 1):
        target = (pair + step) % pairs
        other = lax.ppermute(block(2 * target + 1 - core), "blk", swap)
        total = lax.optimization_barrier(block(2 * target + core)) + other
        if step < pairs:
            route = [(i, (i + 2 * step) % members) for i in range(members)]
            arrived.append(lax.ppermute(total.astype(jnp.bfloat16), "blk", route))
    for part in arrived:
        total = total + part.astype(jnp.float32)
    return total


def shards(entity_table, relations, head_ids, rel_ids, tail_ids, neg_ids):
    owner_count = lax.axis_size("owner")
    cycle_count = lax.axis_size("blk")
    entity_rows, feature_count = entity_table.shape
    triple_count = head_ids.shape[0]
    negative_count = neg_ids.shape[0]
    relation_count = relations.shape[0]
    wanted = jnp.concatenate([head_ids, tail_ids, neg_ids])
    wanted_count = wanted.shape[0]
    capacity = 5 * wanted_count // (2 * owner_count)
    owners = wanted // entity_rows
    local_rows = wanted % entity_rows
    onehot = (owners[:, None] == jnp.arange(owner_count, dtype=jnp.int32)[None, :]).astype(
        jnp.bfloat16
    )
    slot_index = ranks(onehot)
    target = owners * capacity + slot_index
    slots = jnp.arange(owner_count * capacity, dtype=jnp.int32)
    packing = (slots[:, None] == target[None, :]).astype(jnp.bfloat16)
    digits = jnp.stack([local_rows // 64, local_rows % 64], axis=1).astype(jnp.bfloat16)
    packed = jnp.dot(packing, digits, preferred_element_type=jnp.float32).astype(jnp.int32)
    requests = (packed[:, 0] * 64 + packed[:, 1]).reshape(owner_count, capacity)
    asked_rows = lax.all_to_all(requests, "owner", split_axis=0, concat_axis=0, tiled=True)
    found_rows = entity_table.at[asked_rows].get(mode="promise_in_bounds")
    fetched, asked_rows = (
        lax.all_to_all(found_rows, "owner", split_axis=0, concat_axis=0, tiled=True),
        asked_rows,
    )
    fetched_rows = fetched.reshape(owner_count * capacity, feature_count)
    fetched_rows = fetched_rows.at[target].get(mode="promise_in_bounds")
    head_rows = fetched_rows[:triple_count]
    tail_rows = fetched_rows[triple_count : 2 * triple_count]
    negative_rows = fetched_rows[2 * triple_count :]
    routes = [[(i, i ^ step) for i in range(cycle_count)] for step in range(cycle_count)]
    visitors = [negative_rows]
    for step in range(1, cycle_count):
        visitors.append(lax.ppermute(negative_rows, "blk", routes[step]))
    relation_hot = (
        rel_ids[:, None] == jnp.arange(relation_count, dtype=jnp.int32)[None, :]
    ).astype(jnp.bfloat16)
    spread_heads = (head_rows[:, None, :] * relation_hot[:, :, None]).reshape(
        triple_count, relation_count * feature_count
    )
    flat_relations = relations.reshape(relation_count * feature_count, feature_count)
    queries = jnp.dot(spread_heads, flat_relations, preferred_element_type=jnp.float32).astype(
        jnp.bfloat16
    )
    positive = jnp.einsum("id,id->i", queries, tail_rows, preferred_element_type=jnp.float32)
    slopes = -jax.nn.sigmoid(-positive)
    scale_neg = (cycle_count * negative_count) ** (-0.5)
    partner = slopes[:, None] * tail_rows.astype(jnp.float32)
    contract_rows = (((0,), (0,)), ((), ()))
    contract_cols = (((1,), (1,)), ((), ()))
    returning = []
    for step, visitor in enumerate(visitors):
        scores = lax.dot_general(
            queries, visitor, contract_cols, preferred_element_type=jnp.float32
        )
        weights = (scale_neg * jax.nn.sigmoid(scores)).astype(jnp.bfloat16)
        partner = partner + jnp.dot(weights, visitor, preferred_element_type=jnp.float32)
        sums = lax.dot_general(weights, queries, contract_rows, preferred_element_type=jnp.float32)
        if step == 0:
            collected = sums
        else:
            returning.append(lax.ppermute(sums.astype(jnp.bfloat16), "blk", routes[step]))
    partner_low = partner.astype(jnp.bfloat16)
    spread_partner = partner_low[:, None, :] * relation_hot[:, :, None]
    head_grad = jnp.einsum(
        "ire,rde->id", spread_partner, relations, preferred_element_type=jnp.float32
    )
    tail_grad = slopes[:, None] * queries.astype(jnp.float32)
    rel_term = lax.dot_general(
        spread_heads, partner_low, contract_rows, preferred_element_type=jnp.float32
    )
    shares = rel_term.reshape(cycle_count, -1, feature_count)
    me = lax.axis_index("blk")
    share = lax.dynamic_index_in_dim(shares, me, keepdims=False)
    sent = [
        lax.dynamic_index_in_dim(shares, jnp.bitwise_xor(me, step), keepdims=False)
        for step in range(1, cycle_count)
    ]
    for step in range(1, cycle_count):
        part = lax.ppermute(sent[step - 1].astype(jnp.bfloat16), "blk", routes[step])
        share = share + part.astype(jnp.float32)
    relation_rows = share.astype(jnp.bfloat16).reshape(owner_count, -1, feature_count)
    triple_grads = jnp.concatenate([head_grad, tail_grad], axis=0).astype(jnp.bfloat16)
    outgoing = jnp.dot(
        packing[:, : 2 * triple_count], triple_grads, preferred_element_type=jnp.float32
    ).astype(jnp.bfloat16)
    for part in returning:
        collected = collected + part.astype(jnp.float32)
    outgoing = outgoing + jnp.dot(
        packing[:, 2 * triple_count :],
        collected.astype(jnp.bfloat16),
        preferred_element_type=jnp.float32,
    ).astype(jnp.bfloat16)
    outgoing = outgoing.reshape(owner_count, capacity, feature_count)
    outgoing = jnp.concatenate([outgoing, relation_rows], axis=1)
    returned = lax.all_to_all(outgoing, "owner", split_axis=0, concat_axis=0, tiled=True)
    summed_rows = jnp.sum(returned[:, capacity:].astype(jnp.float32), axis=0)
    rel_grad = lax.all_gather(summed_rows, "owner", tiled=True)
    rel_grad = rel_grad.reshape(relation_count // cycle_count, feature_count, feature_count)
    rows = jnp.pad(asked_rows, ((0, 0), (0, relation_rows.shape[1])), constant_values=-1)
    ent_grad = group_sums(rows.reshape(-1), returned.reshape(-1, feature_count), entity_rows)
    return (ent_grad, rel_grad)


def solution(mesh):
    placed = (
        P("owner", None),
        P(),
        P(("owner", "blk")),
        P(("owner", "blk")),
        P(("owner", "blk")),
        P(("owner", "blk")),
    )
    return jax.shard_map(
        shards,
        mesh=mesh,
        in_specs=placed,
        out_specs=(P(("owner", "blk"), None), P("blk", None, None)),
        check_vma=False,
    )
```

```python
import jax
import jax.numpy as jnp
from jax import lax
from jax.sharding import PartitionSpec as P


def earlier(count):
    place = jnp.arange(count, dtype=jnp.int32)
    return (place[:, None] > place[None, :]).astype(jnp.bfloat16)


def ranks(onehot):
    ids, owner_count = onehot.shape
    run = 128
    runs = onehot.reshape(ids // run, run, owner_count)
    within = jnp.einsum("ij,bjo->bio", earlier(run), runs, preferred_element_type=jnp.float32)
    totals = jnp.sum(runs.astype(jnp.float32), axis=1).astype(jnp.bfloat16)
    carried = jnp.dot(earlier(ids // run), totals, preferred_element_type=jnp.float32)
    before = within + carried[:, None, :]
    return jnp.sum(before * runs.astype(jnp.float32), axis=2).reshape(ids).astype(jnp.int32)


def group_sums(rows, grads, entity_rows):
    members = lax.axis_size("blk")
    pairs = members // 2
    size = entity_rows // members
    me = lax.axis_index("blk")
    pair, core = me // 2, me % 2
    swap = [(i, i ^ 1) for i in range(members)]

    def block(index):
        wanted = index * size + jnp.arange(size, dtype=jnp.int32)
        landing = (wanted[:, None] == rows[None, :]).astype(jnp.bfloat16)
        return jnp.dot(landing, grads, preferred_element_type=jnp.float32)

    arrived = []
    for step in range(1, pairs + 1):
        target = (pair + step) % pairs
        other = lax.ppermute(block(2 * target + 1 - core), "blk", swap)
        total = lax.optimization_barrier(block(2 * target + core)) + other
        if step < pairs:
            route = [(i, (i + 2 * step) % members) for i in range(members)]
            arrived.append(lax.ppermute(total.astype(jnp.bfloat16), "blk", route))
    for part in arrived:
        total = total + part.astype(jnp.float32)
    return total


def shards(entity_table, relations, head_ids, rel_ids, tail_ids, neg_ids):
    owner_count = lax.axis_size("owner")
    cycle_count = lax.axis_size("blk")
    entity_rows, feature_count = entity_table.shape
    triple_count = head_ids.shape[0]
    negative_count = neg_ids.shape[0]
    relation_count = relations.shape[0]
    wanted = jnp.concatenate([head_ids, tail_ids, neg_ids])
    wanted_count = wanted.shape[0]
    capacity = 5 * wanted_count // (2 * owner_count)
    owners = wanted // entity_rows
    local_rows = wanted % entity_rows
    onehot = (owners[:, None] == jnp.arange(owner_count, dtype=jnp.int32)[None, :]).astype(
        jnp.bfloat16
    )
    slot_index = ranks(onehot)
    target = owners * capacity + slot_index
    slots = jnp.arange(owner_count * capacity, dtype=jnp.int32)
    packing = (slots[:, None] == target[None, :]).astype(jnp.bfloat16)
    digits = jnp.stack([local_rows // 64, local_rows % 64], axis=1).astype(jnp.bfloat16)
    packed = jnp.dot(packing, digits, preferred_element_type=jnp.float32).astype(jnp.int32)
    requests = (packed[:, 0] * 64 + packed[:, 1]).reshape(owner_count, capacity)
    asked_rows = lax.all_to_all(requests, "owner", split_axis=0, concat_axis=0, tiled=True)
    found_rows = entity_table.at[asked_rows].get(mode="promise_in_bounds")
    fetched, asked_rows = (
        lax.all_to_all(found_rows, "owner", split_axis=0, concat_axis=0, tiled=True),
        asked_rows,
    )
    fetched_rows = fetched.reshape(owner_count * capacity, feature_count)
    fetched_rows = fetched_rows.at[target].get(mode="promise_in_bounds")
    head_rows = fetched_rows[:triple_count]
    tail_rows = fetched_rows[triple_count : 2 * triple_count]
    negative_rows = fetched_rows[2 * triple_count :]
    routes = [[(i, i ^ step) for i in range(cycle_count)] for step in range(cycle_count)]
    visitors = [negative_rows]
    for step in range(1, cycle_count):
        visitors.append(lax.ppermute(negative_rows, "blk", routes[step]))
    relation_hot = (
        rel_ids[:, None] == jnp.arange(relation_count, dtype=jnp.int32)[None, :]
    ).astype(jnp.bfloat16)
    spread_heads = (head_rows[:, None, :] * relation_hot[:, :, None]).reshape(
        triple_count, relation_count * feature_count
    )
    flat_relations = relations.reshape(relation_count * feature_count, feature_count)
    queries = jnp.dot(spread_heads, flat_relations, preferred_element_type=jnp.float32).astype(
        jnp.bfloat16
    )
    positive = jnp.einsum("id,id->i", queries, tail_rows, preferred_element_type=jnp.float32)
    slopes = -jax.nn.sigmoid(-positive)
    scale_neg = (cycle_count * negative_count) ** (-0.5)
    partner = slopes[:, None] * tail_rows.astype(jnp.float32)
    contract_rows = (((0,), (0,)), ((), ()))
    contract_cols = (((1,), (1,)), ((), ()))
    returning = []
    for step, visitor in enumerate(visitors):
        scores = lax.dot_general(
            queries, visitor, contract_cols, preferred_element_type=jnp.float32
        )
        weights = (scale_neg * jax.nn.sigmoid(scores)).astype(jnp.bfloat16)
        partner = partner + jnp.dot(weights, visitor, preferred_element_type=jnp.float32)
        sums = lax.dot_general(weights, queries, contract_rows, preferred_element_type=jnp.float32)
        if step == 0:
            collected = sums
        else:
            returning.append(lax.ppermute(sums.astype(jnp.bfloat16), "blk", routes[step]))
    partner_low = partner.astype(jnp.bfloat16)
    spread_partner = partner_low[:, None, :] * relation_hot[:, :, None]
    head_grad = jnp.einsum(
        "ire,rde->id", spread_partner, relations, preferred_element_type=jnp.float32
    )
    tail_grad = slopes[:, None] * queries.astype(jnp.float32)
    rel_term = lax.dot_general(
        spread_heads, partner_low, contract_rows, preferred_element_type=jnp.float32
    )
    shares = rel_term.reshape(cycle_count, -1, feature_count)
    me = lax.axis_index("blk")
    share = lax.dynamic_index_in_dim(shares, me, keepdims=False)
    sent = [
        lax.dynamic_index_in_dim(shares, jnp.bitwise_xor(me, step), keepdims=False)
        for step in range(1, cycle_count)
    ]
    for step in range(1, cycle_count):
        part = lax.ppermute(sent[step - 1].astype(jnp.bfloat16), "blk", routes[step])
        share = share + part.astype(jnp.float32)
    relation_rows = share.astype(jnp.bfloat16).reshape(owner_count, -1, feature_count)
    triple_grads = jnp.concatenate([head_grad, tail_grad], axis=0).astype(jnp.bfloat16)
    outgoing = jnp.dot(
        packing[:, : 2 * triple_count], triple_grads, preferred_element_type=jnp.float32
    ).astype(jnp.bfloat16)
    for part in returning:
        collected = collected + part.astype(jnp.float32)
    outgoing = outgoing + jnp.dot(
        packing[:, 2 * triple_count :],
        collected.astype(jnp.bfloat16),
        preferred_element_type=jnp.float32,
    ).astype(jnp.bfloat16)
    outgoing = outgoing.reshape(owner_count, capacity, feature_count)
    outgoing = jnp.concatenate([outgoing, relation_rows], axis=1)
    returned = lax.all_to_all(outgoing, "owner", split_axis=0, concat_axis=0, tiled=True)
    summed_rows = jnp.sum(returned[:, capacity:].astype(jnp.float32), axis=0)
    holder = lax.axis_index("owner")
    rel_grad = jnp.zeros((owner_count, *summed_rows.shape), jnp.float32)
    for step in range(owner_count):
        piece = summed_rows
        if step > 0:
            piece = lax.ppermute(piece, "owner", [(i, i ^ step) for i in range(owner_count)])
        rel_grad = lax.dynamic_update_index_in_dim(
            rel_grad, piece, jnp.bitwise_xor(holder, step), 0
        )
    rel_grad = rel_grad.reshape(relation_count // cycle_count, feature_count, feature_count)
    rows = jnp.pad(asked_rows, ((0, 0), (0, relation_rows.shape[1])), constant_values=-1)
    ent_grad = group_sums(rows.reshape(-1), returned.reshape(-1, feature_count), entity_rows)
    return (ent_grad, rel_grad)


def solution(mesh):
    placed = (
        P("owner", None),
        P(),
        P(("owner", "blk")),
        P(("owner", "blk")),
        P(("owner", "blk")),
        P(("owner", "blk")),
    )
    return jax.shard_map(
        shards,
        mesh=mesh,
        in_specs=placed,
        out_specs=(P(("owner", "blk"), None), P("blk", None, None)),
        check_vma=False,
    )
```
